32 devices in a mesh: seq: 8 (over z, y), grp: 4 (over x, core).
Axes of the slice: x: 2, y: 2, z: 4, core: 2. Of those that a mesh axis runs over, the one named last changes fastest.
Arguments:
- query: bfloat16 [4, 1024, 2048], P('grp', 'seq'), may hold values from -6 to 6
- key_in: bfloat16 [4, 1024, 2048], P('grp', 'seq'), may hold values from -6 to 6
- value: bfloat16 [4, 1024, 2048], P('grp', 'seq'), may hold values from -6 to 6
- cotangent: bfloat16 [4, 1024, 2048], P('grp', 'seq'), may hold values from -6 to 6
- routes: int32 [4, 1024, 6], P('grp', 'seq'), may hold values from 0 to 15, as said below
- gates: float32 [4, 1024, 6], P('grp', 'seq'), may hold values from 0.01 to 0.1
- hidden: bfloat16 [4, 1024, 6, 704], P('grp', 'seq'), may hold values from -6 to 6
Outputs:
- attention_out: bfloat16 [4, 1024, 2048], P('grp', 'seq')
- grad_query: bfloat16 [4, 1024, 2048], P('grp', 'seq')
- grad_key: bfloat16 [4, 1024, 2048], P('grp', 'seq')
- grad_value: bfloat16 [4, 1024, 2048], P('grp', 'seq')
- expert_grad: bfloat16 [16, 704, 2048], P('seq', 'grp')
The draws below stay inside these ranges and needn't reach their ends.
Inputs may be any that keep to these rules, and one draw needn't show every extreme that they name: `routes`: the 6 experts of a token differ. Among the 128 tokens of one device (aligned blocks of the positions of a sequence) no expert is named more than 128 times, and in every sequence some expert is named exactly 128 times by the tokens of each device. Expert ids are small integers and may be packed several to a word whenever they are sent.
All inputs are finite; a program needn't handle non-finite values.
Results may differ from the reference program's by a relative error of at most 0.04.
Values may be sent and summed in bfloat16 or wider, within the bound.
A program may use at most 192 MiB of HBM per device.

```python
import math
import jax
import jax.numpy as jnp
from jax import lax

HEADS = 16
DH = 128
F = 704
TOPK = 6
TOK_DEV = 128
DW = 2048
EXPERTS = 16
SEQS = 4
LENGTH = 1024
CAP = 128
N_SEQ = 8


def draw_routes(key, part):
    per_seq = LENGTH // TOK_DEV
    blocks = SEQS * per_seq
    slots = TOK_DEV * TOPK
    seq_keys = jax.random.split(jax.random.fold_in(key, 11), SEQS)
    hot_seq = jax.vmap(lambda single: jax.random.randint(single, (), 0, EXPERTS))(seq_keys)
    block_keys = jax.random.split(jax.random.fold_in(key, 17), blocks)
    hot_block = jnp.repeat(hot_seq, per_seq)

    def one_block(block_key, hottest):
        keys = jax.random.split(block_key, 5)
        order = jax.random.permutation(keys[0], EXPERTS)
        table = order[jnp.arange(slots) % EXPERTS].reshape(TOK_DEV, TOPK)
        has_hot = jnp.any(table == hottest, axis=1)
        base_hot = jnp.sum((table == hottest).astype(jnp.int32))
        free_rows = jnp.logical_not(has_hot)
        ranking = jnp.cumsum(free_rows.astype(jnp.int32))
        chosen = free_rows & (ranking <= CAP - base_hot)
        table = table.at[:, 0].set(jnp.where(chosen, hottest, table[:, 0]))
        second = (hottest + 1 + jax.random.randint(keys[1], (), 0, EXPERTS - 1)) % EXPERTS
        has_second = jnp.any(table == second, axis=1)
        now_hot = jnp.any(table == hottest, axis=1)
        base_second = jnp.sum((table == second).astype(jnp.int32))
        extra = jax.random.randint(keys[2], (), 0, CAP - base_second + 1)
        free_two = jnp.logical_not(has_second) & jnp.logical_not(now_hot)
        ranking_two = jnp.cumsum(free_two.astype(jnp.int32))
        chosen_two = free_two & (ranking_two <= extra)
        table = table.at[:, 1].set(jnp.where(chosen_two, second, table[:, 1]))
        shuffle = jax.random.permutation(keys[3], TOK_DEV)
        table = table[shuffle]
        rolls = jax.random.randint(keys[4], (TOK_DEV,), 0, TOPK)
        columns = (jnp.arange(TOPK)[None, :] + rolls[:, None]) % TOPK
        return jnp.take_along_axis(table, columns, axis=1)
    result = jax.vmap(one_block)(block_keys, hot_block)
    return result.reshape(SEQS, LENGTH, TOPK).astype(jnp.int32)


def block_levels(rng, extent, cuts, smallest, high):
    loudness = 1.0
    for dim, shards_of in cuts:
        draws = jax.random.uniform(jax.random.fold_in(jax.random.fold_in(rng, 6), dim), (shards_of,), jnp.float32, smallest / len(cuts), high / len(cuts))
        loudness = loudness * jnp.repeat(jnp.exp(draws), extent[dim] // shards_of).reshape((-1,) + (1,) * (len(extent) - 1 - dim))
    return loudness


def normal_values(own_key, dims, scale, bound, pieces=(), kind=jnp.bfloat16):
    values = jax.random.normal(own_key, dims, jnp.float32) * scale
    if len(pieces) > 0:
        values = block_levels(own_key, dims, pieces, -0.22, 0.18) * values
    return jnp.clip(values, min=-bound, max=bound).astype(kind)


def setup_inputs(seed: int = 0) -> dict:
    key_list = jax.random.split(jax.random.key(seed), 8)
    return {
        "query": normal_values(key_list[0], (SEQS, LENGTH, DW), 1.0, 6.0, ((0, 4), (1, 8))),
        "key_in": normal_values(key_list[1], (SEQS, LENGTH, DW), 1.0, 6.0, ((0, 4), (1, 8))),
        "value": normal_values(key_list[2], (SEQS, LENGTH, DW), 1.0, 6.0, ((0, 4), (1, 8))),
        "cotangent": normal_values(key_list[3], (SEQS, LENGTH, DW), 1.0, 6.0, ((0, 4), (1, 8))),
        "routes": draw_routes(jax.random.fold_in(key_list[7], 71), 0),
        "gates": jnp.clip(jnp.exp(math.log(0.1) - 2.3025851 * jax.random.uniform(key_list[5], (SEQS, LENGTH, TOPK), jnp.float32) ** block_levels(key_list[5], (SEQS, LENGTH, TOPK), ((0, 4), (1, 8)), -0.2, 0.2)), 0.01, 0.1),
        "hidden": normal_values(key_list[6], (SEQS, LENGTH, TOPK, F), 1.0, 6.0, ((0, 4), (1, 8))),
    }


PRECISE = lax.Precision.HIGHEST

def attention_pass(query, key_in, value, cotangent):
    blocks = LENGTH // TOK_DEV

    def split_heads(array):
        return array.astype(jnp.float32).reshape(SEQS, blocks, TOK_DEV, HEADS, DH).transpose(1, 0, 2, 3, 4)
    query_full = split_heads(query)
    key_full = split_heads(key_in)
    value_full = split_heads(value)
    grad_out = split_heads(cotangent)
    position = jnp.arange(LENGTH, dtype=jnp.int32).reshape(blocks, TOK_DEV)
    scaling = 1.0 / jnp.sqrt(DH * (position + 1).astype(jnp.float32))
    causal = jnp.tril(jnp.ones((TOK_DEV, TOK_DEV), jnp.float32))

    def forward_step(prefix_state, inputs):
        query_blk, key_blk, value_blk, grad_blk, scale_blk = inputs
        row_scale = scale_blk[None, :, None, None]
        scores = jnp.einsum('sthd,suhd->shtu', query_blk, key_blk, precision=PRECISE) * causal
        outputs = jnp.einsum('shtu,suhe->sthe', scores, value_blk, precision=PRECISE)
        outputs = (outputs + jnp.einsum('sthd,shde->sthe', query_blk, prefix_state, precision=PRECISE)) * row_scale
        grad_scores = jnp.einsum('sthe,suhe->shtu', grad_blk, value_blk, precision=PRECISE) * causal
        grad_q = jnp.einsum('shtu,suhd->sthd', grad_scores, key_blk, precision=PRECISE)
        grad_q = (grad_q + jnp.einsum('sthe,shde->sthd', grad_blk, prefix_state, precision=PRECISE)) * row_scale
        new_state = prefix_state + jnp.einsum('suhd,suhe->shde', key_blk, value_blk, precision=PRECISE)
        return (new_state, (outputs, grad_q))

    def backward_step(after_state, inputs):
        query_blk, key_blk, value_blk, grad_blk, scale_blk = inputs
        col_scale = scale_blk[None, None, :, None]
        weighted = jnp.einsum('sthd,suhd->shtu', query_blk, key_blk, precision=PRECISE) * causal * col_scale
        grad_weighted = jnp.einsum('sthe,suhe->shtu', grad_blk, value_blk, precision=PRECISE) * causal * col_scale
        grad_k = jnp.einsum('shtu,sthd->suhd', grad_weighted, query_blk, precision=PRECISE)
        grad_k = grad_k + jnp.einsum('suhe,shde->suhd', value_blk, after_state, precision=PRECISE)
        grad_v = jnp.einsum('shtu,sthe->suhe', weighted, grad_blk, precision=PRECISE)
        grad_v = grad_v + jnp.einsum('suhd,shde->suhe', key_blk, after_state, precision=PRECISE)
        scaled_query = query_blk * scale_blk[None, :, None, None]
        new_state = after_state + jnp.einsum('sthd,sthe->shde', scaled_query, grad_blk, precision=PRECISE)
        return (new_state, (grad_k, grad_v))
    empty = jnp.zeros((SEQS, HEADS, DH, DH), jnp.float32)
    inputs = (query_full, key_full, value_full, grad_out, scaling)
    final_fwd, (outputs, grad_q) = lax.scan(forward_step, empty, inputs)
    final_bwd, (grad_k, grad_v) = lax.scan(backward_step, empty, inputs, reverse=True)

    def join_heads(array):
        return array.transpose(1, 0, 2, 3, 4).reshape(SEQS, LENGTH, HEADS * DH).astype(jnp.bfloat16)
    return (join_heads(outputs), join_heads(grad_q), join_heads(grad_k), join_heads(grad_v))

def group_gradient(route_seq, gate_seq, hidden_seq, cot_seq):
    count = LENGTH * TOPK
    span = N_SEQ * CAP
    flat_ids = route_seq.reshape(count).astype(jnp.int32)
    scaled = (gate_seq.reshape(count, 1) * hidden_seq.reshape(count, F).astype(jnp.float32)).astype(jnp.bfloat16)
    order = jnp.argsort(flat_ids, stable=True).astype(jnp.int32)
    sorted_ids = flat_ids[order]
    expert_ids = jnp.arange(EXPERTS, dtype=jnp.int32)
    starts = jnp.searchsorted(sorted_ids, expert_ids, side='left').astype(jnp.int32)
    ends = jnp.searchsorted(sorted_ids, expert_ids, side='right').astype(jnp.int32)
    sorted_rows = jnp.concatenate([scaled[order], jnp.zeros((span, F), jnp.bfloat16)], axis=0)
    sorted_tokens = jnp.concatenate([order // TOPK, jnp.zeros((span,), jnp.int32)], axis=0).astype(jnp.int32)

    def one_expert(expert):
        start = starts[expert]
        rows_h = lax.dynamic_slice_in_dim(sorted_rows, start, span, 0)
        rows_t = lax.dynamic_slice_in_dim(sorted_tokens, start, span, 0)
        live = jnp.arange(span, dtype=jnp.int32) < ends[expert] - start
        rows_h = jnp.where(live[:, None], rows_h.astype(jnp.float32), 0.0)
        rows_d = jnp.take(cot_seq, rows_t, axis=0).astype(jnp.float32)
        return jnp.dot(rows_h.T, rows_d, preferred_element_type=jnp.float32)
    return lax.map(one_expert, expert_ids)

def reference(query, key_in, value, cotangent, routes, gates, hidden):
    attention_out, grad_query, grad_key, grad_value = attention_pass(query, key_in, value, cotangent)

    def accumulate(total, inputs):
        partial_sum = group_gradient(*inputs)
        rounded = lax.optimization_barrier(partial_sum.astype(jnp.bfloat16)).astype(jnp.float32)
        return (total + rounded, jnp.zeros((), jnp.float32))
    start_total = jnp.zeros((EXPERTS, F, HEADS * DH), jnp.float32)
    summed, unused = lax.scan(accumulate, start_total, (routes, gates, hidden, cotangent))
    expert_grad = summed.astype(jnp.bfloat16)
    return (attention_out, grad_query, grad_key, grad_value, expert_grad)
```

```python
import functools

import jax
import jax.numpy as jnp
from jax import lax
from jax.experimental import pallas as pl
from jax.experimental.pallas import tpu as pltpu
from jax.sharding import PartitionSpec as P

HEADS = 16
EXP_DEV = 2
BF = jnp.bfloat16
F32 = jnp.float32
VMEM_BYTES = 56 * 1024 * 1024


def dot(a, b, ca, cb):
    return lax.dot_general(a, b, (((ca,), (cb,)), ((), ())), preferred_element_type=F32)


def exchange_kernel(
    inner,
    q_ref, k_ref, v_ref, g_ref, hid_ref, routes_ref,
    out_ref, gq_ref, gk_ref, gv_ref, cotg_ref, arr_ref,
    slots, own_state, peer_state, total_state, chain_in, chain_out, carried, score_ref, gscore_ref,
    cot_send, cot_recv, slot_send, slot_recv, st_send, st_recv, ch_send, ch_recv, local_sem,
):
    count = lax.axis_size("seq")
    outer = count // inner
    me = lax.axis_index("seq")
    row = me // inner
    col = me % inner
    tokens = q_ref.shape[0]
    topk = hid_ref.shape[0]
    head = q_ref.shape[1] // HEADS

    def remote(src, dst, send, recv, target):
        return pltpu.make_async_remote_copy(
            src_ref=src, dst_ref=dst, send_sem=send, recv_sem=recv,
            device_id={"seq": target}, device_id_type=pl.DeviceIdType.MESH,
        )

    barrier = pltpu.get_barrier_semaphore()

    def greet(step, carry):
        pl.semaphore_signal(
            barrier, inc=1, device_id={"seq": lax.rem(me + step, count)},
            device_id_type=pl.DeviceIdType.MESH,
        )
        return carry

    lax.fori_loop(1, count, greet, 0)
    pl.semaphore_wait(barrier, count - 1)

    def cot_copy(origin, src, lane, target):
        return remote(src, cotg_ref.at[origin], cot_send.at[origin, lane], cot_recv.at[origin], target)

    def cot_spread(origin, src, up, down, act):
        if up is not None:
            @pl.when(up)
            def _():
                act(cot_copy(origin, src, 0, me + inner))
        if down is not None:
            @pl.when(down)
            def _():
                act(cot_copy(origin, src, 1, me - inner))
        for off in range(1, inner):
            act(cot_copy(origin, src, 1 + off, row * inner + lax.rem(col + off, inner)))

    def cot_forward(step, act, wait):
        @pl.when(row >= step)
        def _():
            origin = me - step * inner
            if wait:
                cot_copy(origin, cotg_ref.at[origin], 0, origin).wait_recv()
            cot_spread(origin, cotg_ref.at[origin], row + 1 < outer, None, act)

        @pl.when(row + step < outer)
        def _():
            origin = me + step * inner
            if wait:
                cot_copy(origin, cotg_ref.at[origin], 0, origin).wait_recv()
            cot_spread(origin, cotg_ref.at[origin], None, row >= 1, act)

    start = lambda copy: copy.start()
    finish = lambda copy: copy.wait_send()

    cot_spread(me, g_ref, row + 1 < outer, row >= 1, start)
    own_cot = pltpu.make_async_copy(g_ref, cotg_ref.at[me], local_sem.at[0])
    own_cot.start()

    position = me * tokens + lax.broadcasted_iota(jnp.int32, (tokens, 1), 0)
    scaling = lax.rsqrt((head * (position + 1)).astype(F32))
    causal = lax.broadcasted_iota(jnp.int32, (tokens, tokens), 0) >= lax.broadcasted_iota(
        jnp.int32, (tokens, tokens), 1
    )

    def heads_of(h):
        return pl.ds(pl.multiple_of(h * head, head), head)

    def states(h, carry):
        at = heads_of(h)
        q, k, v, g = q_ref[:, at], k_ref[:, at], v_ref[:, at], g_ref[:, at]
        own_state[0, at, :] = dot(k, v, 0, 0).astype(BF)
        own_state[1, at, :] = dot((q.astype(F32) * scaling).astype(BF), g, 0, 0).astype(BF)
        return carry

    lax.fori_loop(0, HEADS, states, 0)

    def state_copy(off):
        return remote(
            own_state, peer_state.at[col], st_send.at[off], st_recv.at[col],
            row * inner + lax.rem(col + off, inner),
        )

    for off in range(1, inner):
        state_copy(off).start()

    def fill(target):
        for x in range(EXP_DEV):
            expert = target * EXP_DEV + x
            total = jnp.zeros((tokens, hid_ref.shape[2]), F32)
            for j in range(topk):
                chosen = routes_ref[:, j : j + 1] == expert
                total = total + jnp.where(chosen, hid_ref[j].astype(F32), 0.0)
            slots[target, x] = total.astype(BF)

    def slot_copy(off):
        target = lax.rem(me + off, count)
        return remote(
            slots.at[target], arr_ref.at[:, pl.ds(pl.multiple_of(me * tokens, tokens), tokens), :],
            slot_send.at[off], slot_recv.at[me], target,
        )

    def send_slots(off, carry):
        fill(lax.rem(me + off, count))
        slot_copy(off).start()
        return carry

    lax.fori_loop(1, count, send_slots, 0)
    fill(me)
    own_slots = pltpu.make_async_copy(
        slots.at[me], arr_ref.at[:, pl.ds(pl.multiple_of(me * tokens, tokens), tokens), :],
        local_sem.at[1],
    )
    own_slots.start()

    def state_wait(off):
        source = lax.rem(col + off, inner)
        remote(
            own_state, peer_state.at[source], st_send.at[off], st_recv.at[source],
            row * inner + source,
        ).wait_recv()

    for off in range(1, inner):
        state_wait(off)
    peer_state[col] = own_state[...]

    def sum_rows(h, carry):
        at = heads_of(h)
        for which in range(2):
            total = jnp.zeros((head, head), F32)
            part = jnp.zeros((head, head), F32)
            for c in range(inner):
                block = peer_state[c, which, at, :].astype(F32)
                total = total + block
                counts = (c < col) if which == 0 else (c > col)
                part = part + jnp.where(counts, block, 0.0)
            total_state[which, at, :] = total
            carried[which, at, :] = part
        return carry

    lax.fori_loop(0, HEADS, sum_rows, 0)

    def chain_copy(which):
        target = me + inner if which == 0 else me - inner
        return remote(
            chain_out.at[which], chain_in.at[which], ch_send.at[which], ch_recv.at[which], target
        )

    def chain_step(which, first, last):
        if not first:
            chain_copy(which).wait_recv()

        def one(h, carry):
            at = heads_of(h)
            here = total_state[which, at, :]
            if not first:
                before = chain_in[which, at, :].astype(F32)
                carried[which, at, :] = carried[which, at, :] + before
                here = here + before
            if not last:
                chain_out[which, at, :] = here.astype(BF)
            return carry

        lax.fori_loop(0, HEADS, one, 0)
        if not last:
            chain_copy(which).start()

    def local_scores(h, carry):
        at = heads_of(h)
        q, k, v, g = q_ref[:, at], k_ref[:, at], v_ref[:, at], g_ref[:, at]
        score_ref[h] = jnp.where(causal, dot(q, k, 1, 1), 0.0).astype(BF)
        gscore_ref[h] = jnp.where(causal, dot(g, v, 1, 1), 0.0).astype(BF)
        return carry

    for step in range(outer):
        @pl.when(row == step)
        def _():
            chain_step(0, step == 0, step == outer - 1)

        @pl.when(row == outer - 1 - step)
        def _():
            chain_step(1, step == 0, step == outer - 1)

        if step == 0:
            lax.fori_loop(0, HEADS, local_scores, 0)
        if step >= 1:
            cot_forward(step, start, True)

    def finals(h, carry):
        at = heads_of(h)
        q, k, v, g = q_ref[:, at], k_ref[:, at], v_ref[:, at], g_ref[:, at]
        before = carried[0, at, :].astype(BF)
        after = carried[1, at, :].astype(BF)
        scores = score_ref[h]
        gscores = gscore_ref[h]
        weighted = (scores.astype(F32) * scaling).astype(BF)
        gweighted = (gscores.astype(F32) * scaling).astype(BF)
        out_ref[:, at] = ((dot(scores, v, 1, 0) + dot(q, before, 1, 0)) * scaling).astype(BF)
        gq_ref[:, at] = ((dot(gscores, k, 1, 0) + dot(g, before, 1, 1)) * scaling).astype(BF)
        gk_ref[:, at] = (dot(gweighted, q, 0, 0) + dot(v, after, 1, 1)).astype(BF)
        gv_ref[:, at] = (dot(weighted, g, 0, 0) + dot(k, after, 1, 0)).astype(BF)
        return carry

    lax.fori_loop(0, HEADS, finals, 0)

    def cot_last(off, carry):
        source = lax.rem(col + off, inner)

        def one(line, carry):
            origin = line * inner + source
            cot_copy(origin, cotg_ref.at[origin], 0, row * inner + source).wait_recv()
            return carry

        return lax.fori_loop(0, outer, one, carry)

    lax.fori_loop(1, inner, cot_last, 0)

    def slots_last(off, carry):
        source = lax.rem(me + off, count)
        remote(
            slots.at[source],
            arr_ref.at[:, pl.ds(pl.multiple_of(source * tokens, tokens), tokens), :],
            slot_send.at[off], slot_recv.at[source], source,
        ).wait_recv()
        slot_copy(off).wait_send()
        return carry

    lax.fori_loop(1, count, slots_last, 0)
    own_cot.wait()
    own_slots.wait()
    cot_spread(me, g_ref, row + 1 < outer, row >= 1, finish)
    for step in range(1, outer):
        cot_forward(step, finish, False)
    for off in range(1, inner):
        state_copy(off).wait_send()

    @pl.when(row < outer - 1)
    def _():
        chain_copy(0).wait_send()

    @pl.when(row >= 1)
    def _():
        chain_copy(1).wait_send()


def exchange(query, key_in, value, cotangent, hidden, routes):
    count = lax.axis_size("seq")
    inner = 2 if count <= 8 else 8
    tokens, width = query.shape
    head = width // HEADS
    units = hidden.shape[2]
    vmem = pl.BlockSpec(memory_space=pltpu.VMEM)
    anywhere = pl.BlockSpec(memory_space=pl.ANY)
    flat = jax.ShapeDtypeStruct((tokens, width), BF)
    dma = pltpu.SemaphoreType.DMA
    return pl.pallas_call(
        functools.partial(exchange_kernel, inner),
        out_shape=(
            flat, flat, flat, flat,
            jax.ShapeDtypeStruct((count, tokens, width), BF),
            jax.ShapeDtypeStruct((EXP_DEV, count * tokens, units), BF),
        ),
        in_specs=[vmem] * 6,
        out_specs=(vmem, vmem, vmem, vmem, anywhere, anywhere),
        scratch_shapes=[
            pltpu.VMEM((count, EXP_DEV, tokens, units), BF),
            pltpu.VMEM((2, width, head), BF),
            pltpu.VMEM((inner, 2, width, head), BF),
            pltpu.VMEM((2, width, head), F32),
            pltpu.VMEM((2, width, head), BF),
            pltpu.VMEM((2, width, head), BF),
            pltpu.VMEM((2, width, head), F32),
            pltpu.VMEM((HEADS, tokens, tokens), BF),
            pltpu.VMEM((HEADS, tokens, tokens), BF),
            dma((count, inner + 1)), dma((count,)),
            dma((count,)), dma((count,)),
            dma((inner,)), dma((inner,)),
            dma((2,)), dma((2,)),
            dma((2,)),
        ],
        compiler_params=pltpu.CompilerParams(
            collective_id=0, has_side_effects=True, vmem_limit_bytes=VMEM_BYTES
        ),
        name="exchange",
    )(query, key_in, value, cotangent, hidden, routes)


def per_device(query, key_in, value, cotangent, routes, gates, hidden):
    scaled = (gates[0][:, :, None] * hidden[0].astype(F32)).astype(BF).transpose(1, 0, 2)
    outputs, grad_q, grad_k, grad_v, all_cot, arrived = exchange(
        query[0], key_in[0], value[0], cotangent[0], scaled, routes[0]
    )
    all_cot = all_cot.reshape(-1, all_cot.shape[2])
    group_term = jnp.einsum("xtf,td->xfd", arrived, all_cot, preferred_element_type=F32)
    expert_grad = lax.psum_scatter(
        group_term.astype(BF), "grp", scatter_dimension=1, tiled=True
    )
    return (outputs[None], grad_q[None], grad_k[None], grad_v[None], expert_grad)


def solution(mesh):
    rows = P("grp", "seq", None)
    in_specs = (rows, rows, rows, rows, rows, rows, P("grp", "seq", None, None))
    out_specs = (rows, rows, rows, rows, P("seq", "grp", None))
    return jax.shard_map(
        per_device, mesh=mesh, in_specs=in_specs, out_specs=out_specs, check_vma=False
    )
```

```python
import functools

import jax
import jax.numpy as jnp
from jax import lax
from jax.experimental import pallas as pl
from jax.experimental.pallas import tpu as pltpu
from jax.sharding import PartitionSpec as P

HEADS = 16
EXP_DEV = 2
BF = jnp.bfloat16
F32 = jnp.float32
VMEM_BYTES = 56 * 1024 * 1024


def dot(a, b, ca, cb):
    return lax.dot_general(a, b, (((ca,), (cb,)), ((), ())), preferred_element_type=F32)


def exchange_kernel(
    inner, pieces, fused,
    q_ref, k_ref, v_ref, g_ref, hid_ref, routes_ref,
    out_ref, gq_ref, gk_ref, gv_ref, *rest,
):
    if fused:
        grad_ref, *rest = rest
        *rest, group, near_in, far_out, far_in, near_send, near_recv, far_send, far_recv = rest
    (
        cotg_ref, arr_ref, slots, own_state, peer_state, total_state, chain_in, chain_out, carried,
        score_ref, gscore_ref, cot_send, cot_recv, slot_send, slot_recv, st_send, st_recv,
        ch_send, ch_recv, local_sem,
    ) = rest
    count = lax.axis_size("seq")
    outer = count // inner
    me = lax.axis_index("seq")
    row = me // inner
    col = me % inner
    tokens = q_ref.shape[0]
    topk = hid_ref.shape[0]
    width = q_ref.shape[1]
    head = width // HEADS
    piece = width // pieces

    def remote(src, dst, send, recv, target, axis="seq"):
        return pltpu.make_async_remote_copy(
            src_ref=src, dst_ref=dst, send_sem=send, recv_sem=recv,
            device_id={axis: target}, device_id_type=pl.DeviceIdType.MESH,
        )

    if fused:
        grp = lax.axis_index("grp")
        chips = lax.axis_size("grp") // 2
        chip = grp // 2
        core = grp % 2
        sibling = chip * 2 + 1 - core
        far = [lax.rem(chip + off, chips) for off in range(1, chips)]

    barrier = pltpu.get_barrier_semaphore()

    def greet(step, carry):
        pl.semaphore_signal(
            barrier, inc=1, device_id={"seq": lax.rem(me + step, count)},
            device_id_type=pl.DeviceIdType.MESH,
        )
        return carry

    lax.fori_loop(1, count, greet, 0)
    greeted = count - 1
    if fused:
        for other in [sibling] + [x * 2 + core for x in far]:
            pl.semaphore_signal(
                barrier, inc=1, device_id={"grp": other}, device_id_type=pl.DeviceIdType.MESH
            )
        greeted += chips
    pl.semaphore_wait(barrier, greeted)

    def cot_at(c, origin):
        return cotg_ref.at[c, pl.ds(pl.multiple_of(origin * tokens, tokens), tokens), :]

    def own_piece(c):
        return g_ref.at[:, pl.ds(c * piece, piece)]

    def cot_copy(c, origin, src, lane, target):
        return remote(
            src, cot_at(c, origin), cot_send.at[c, origin, lane], cot_recv.at[c, origin], target
        )

    def cot_spread(c, origin, src, up, down, act):
        if up is not None:
            @pl.when(up)
            def _():
                act(cot_copy(c, origin, src, 0, me + inner))
        if down is not None:
            @pl.when(down)
            def _():
                act(cot_copy(c, origin, src, 1, me - inner))
        for off in range(1, inner):
            act(cot_copy(c, origin, src, 1 + off, row * inner + lax.rem(col + off, inner)))

    def cot_own(c, act):
        cot_spread(c, me, own_piece(c), row + 1 < outer, row >= 1, act)

    def cot_forward(c, step, act, wait):
        @pl.when(row >= step)
        def _():
            origin = me - step * inner
            if wait:
                cot_copy(c, origin, cot_at(c, origin), 0, origin).wait_recv()
            cot_spread(c, origin, cot_at(c, origin), row + 1 < outer, None, act)

        @pl.when(row + step < outer)
        def _():
            origin = me + step * inner
            if wait:
                cot_copy(c, origin, cot_at(c, origin), 0, origin).wait_recv()
            cot_spread(c, origin, cot_at(c, origin), None, row >= 1, act)

    start = lambda copy: copy.start()
    finish = lambda copy: copy.wait_send()

    for c in range(min(2, pieces)):
        cot_own(c, start)
    own_cot = [
        pltpu.make_async_copy(own_piece(c), cot_at(c, me), local_sem.at[1 + c])
        for c in range(pieces)
    ]
    for copy in own_cot:
        copy.start()

    position = me * tokens + lax.broadcasted_iota(jnp.int32, (tokens, 1), 0)
    scaling = lax.rsqrt((head * (position + 1)).astype(F32))
    causal = lax.broadcasted_iota(jnp.int32, (tokens, tokens), 0) >= lax.broadcasted_iota(
        jnp.int32, (tokens, tokens), 1
    )

    def heads_of(h):
        return pl.ds(pl.multiple_of(h * head, head), head)

    def states(h, carry):
        at = heads_of(h)
        q, k, v, g = q_ref[:, at], k_ref[:, at], v_ref[:, at], g_ref[:, at]
        own_state[0, at, :] = dot(k, v, 0, 0).astype(BF)
        own_state[1, at, :] = dot((q.astype(F32) * scaling).astype(BF), g, 0, 0).astype(BF)
        return carry

    lax.fori_loop(0, HEADS, states, 0)

    def state_copy(off):
        return remote(
            own_state, peer_state.at[col], st_send.at[off], st_recv.at[col],
            row * inner + lax.rem(col + off, inner),
        )

    for off in range(1, inner):
        state_copy(off).start()

    def fill(target):
        for x in range(EXP_DEV):
            expert = target * EXP_DEV + x
            total = None
            for j in range(topk):
                chosen = jnp.where(routes_ref[j : j + 1, :] == expert, 1.0, 0.0).astype(BF)
                term = hid_ref[j] * chosen
                total = term if total is None else total + term
            slots[target, x] = total

    def arr_at(source):
        return arr_ref.at[:, :, pl.ds(pl.multiple_of(source * tokens, tokens), tokens)]

    def slot_copy(off):
        target = lax.rem(me + off, count)
        return remote(
            slots.at[target], arr_at(me), slot_send.at[off], slot_recv.at[me], target,
        )

    def send_slots(off, carry):
        fill(lax.rem(me + off, count))
        slot_copy(off).start()
        return carry

    lax.fori_loop(1, count, send_slots, 0)
    fill(me)
    own_slots = pltpu.make_async_copy(slots.at[me], arr_at(me), local_sem.at[0])
    own_slots.start()

    def state_wait(off):
        source = lax.rem(col + off, inner)
        remote(
            own_state, peer_state.at[source], st_send.at[off], st_recv.at[source],
            row * inner + source,
        ).wait_recv()

    for off in range(1, inner):
        state_wait(off)
    peer_state[col] = own_state[...]

    def sum_rows(h, carry):
        at = heads_of(h)
        for which in range(2):
            total = jnp.zeros((head, head), F32)
            part = jnp.zeros((head, head), F32)
            for c in range(inner):
                block = peer_state[c, which, at, :].astype(F32)
                total = total + block
                counts = (c < col) if which == 0 else (c > col)
                part = part + jnp.where(counts, block, 0.0)
            total_state[which, at, :] = total
            carried[which, at, :] = part
        return carry

    lax.fori_loop(0, HEADS, sum_rows, 0)

    def chain_copy(which):
        target = me + inner if which == 0 else me - inner
        return remote(
            chain_out.at[which], chain_in.at[which], ch_send.at[which], ch_recv.at[which], target
        )

    def chain_step(which, first, last):
        if not first:
            chain_copy(which).wait_recv()

        def one(h, carry):
            at = heads_of(h)
            here = total_state[which, at, :]
            if not first:
                before = chain_in[which, at, :].astype(F32)
                carried[which, at, :] = carried[which, at, :] + before
                here = here + before
            if not last:
                chain_out[which, at, :] = here.astype(BF)
            return carry

        lax.fori_loop(0, HEADS, one, 0)
        if not last:
            chain_copy(which).start()

    def local_scores(h, carry):
        at = heads_of(h)
        q, k, v, g = q_ref[:, at], k_ref[:, at], v_ref[:, at], g_ref[:, at]
        score_ref[h] = jnp.where(causal, dot(q, k, 1, 1), 0.0).astype(BF)
        gscore_ref[h] = jnp.where(causal, dot(g, v, 1, 1), 0.0).astype(BF)
        return carry

    def advance(c, step):
        if step == 1 and c + 2 < pieces:
            cot_own(c + 2, start)
        cot_forward(c, step, start, True)

    events = [(c, step) for c in range(pieces) for step in range(1, outer)]
    for step in range(outer):
        @pl.when(row == step)
        def _():
            chain_step(0, step == 0, step == outer - 1)

        @pl.when(row == outer - 1 - step)
        def _():
            chain_step(1, step == 0, step == outer - 1)

        if step == 0:
            lax.fori_loop(0, HEADS, local_scores, 0)
        share = len(events) if step == outer - 1 else max(1, len(events) // (outer - step + 1))
        for event in events[:share]:
            advance(*event)
        events = events[share:]

    def finals(h, carry):
        at = heads_of(h)
        q, k, v, g = q_ref[:, at], k_ref[:, at], v_ref[:, at], g_ref[:, at]
        before = carried[0, at, :].astype(BF)
        after = carried[1, at, :].astype(BF)
        scores = score_ref[h]
        gscores = gscore_ref[h]
        weighted = (scores.astype(F32) * scaling).astype(BF)
        gweighted = (gscores.astype(F32) * scaling).astype(BF)
        out_ref[:, at] = ((dot(scores, v, 1, 0) + dot(q, before, 1, 0)) * scaling).astype(BF)
        gq_ref[:, at] = ((dot(gscores, k, 1, 0) + dot(g, before, 1, 1)) * scaling).astype(BF)
        gk_ref[:, at] = (dot(gweighted, q, 0, 0) + dot(v, after, 1, 1)).astype(BF)
        gv_ref[:, at] = (dot(weighted, g, 0, 0) + dot(k, after, 1, 0)).astype(BF)
        return carry

    lax.fori_loop(0, HEADS, finals, 0)

    def slots_last(off, carry):
        source = lax.rem(me + off, count)
        remote(
            slots.at[source], arr_at(source), slot_send.at[off], slot_recv.at[source], source
        ).wait_recv()
        slot_copy(off).wait_send()
        return carry

    lax.fori_loop(1, count, slots_last, 0)
    own_slots.wait()

    def near_copy(c, x):
        return remote(
            group.at[c, :, x * 2 + 1 - core], near_in.at[c, :, x],
            near_send.at[c, x], near_recv.at[c, x], sibling, "grp",
        )

    def far_copy(c, off):
        return remote(
            far_out.at[c, off], far_in.at[c, off], far_send.at[c, off], far_recv.at[c, off],
            far[off] * 2 + core, "grp",
        )

    def pair_sum(c, x, e):
        return group[c, e, x * 2 + core].astype(F32) + near_in[c, e, x].astype(F32)

    def multiply(c):
        quarter = group.shape[3]
        for e in range(EXP_DEV):
            term = dot(arr_ref[e], cotg_ref[c], 1, 0).astype(BF)
            for part in range(2 * chips):
                group[c, e, part] = term[part * quarter : (part + 1) * quarter]
        for x in range(chips):
            near_copy(c, x).start()

    def send_far(c):
        for x in range(chips):
            near_copy(c, x).wait()
        for off in range(chips - 1):
            for e in range(EXP_DEV):
                far_out[c, off, e] = pair_sum(c, far[off], e).astype(BF)
            far_copy(c, off).start()

    def close(c):
        for off in range(chips - 1):
            far_copy(c, off).wait()
        for e in range(EXP_DEV):
            total = pair_sum(c, chip, e)
            for off in range(chips - 1):
                total = total + far_in[c, off, e].astype(F32)
            grad_ref[e, :, pl.ds(c * piece, piece)] = total.astype(BF)

    for c in range(pieces):
        def cot_last(off, carry):
            source = lax.rem(col + off, inner)

            def one(line, carry):
                origin = line * inner + source
                cot_copy(c, origin, cot_at(c, origin), 0, row * inner + source).wait_recv()
                return carry

            return lax.fori_loop(0, outer, one, carry)

        lax.fori_loop(1, inner, cot_last, 0)
        own_cot[c].wait()
        if fused:
            multiply(c)
            if c >= 1:
                send_far(c - 1)
    if fused:
        send_far(pieces - 1)
        for c in range(pieces):
            close(c)

    for c in range(pieces):
        cot_own(c, finish)
        for step in range(1, outer):
            cot_forward(c, step, finish, False)
    for off in range(1, inner):
        state_copy(off).wait_send()

    @pl.when(row < outer - 1)
    def _():
        chain_copy(0).wait_send()

    @pl.when(row >= 1)
    def _():
        chain_copy(1).wait_send()


def exchange(query, key_in, value, cotangent, hidden, routes):
    count = lax.axis_size("seq")
    groups = lax.axis_size("grp")
    inner = 2 if count <= 8 else 8
    fused = count <= 8
    pieces = 4 if fused else 1
    tokens, width = query.shape
    head = width // HEADS
    units = hidden.shape[1]
    chips = groups // 2
    quarter = units // groups
    piece = width // pieces
    vmem = pl.BlockSpec(memory_space=pltpu.VMEM)
    anywhere = pl.BlockSpec(memory_space=pl.ANY)
    flat = jax.ShapeDtypeStruct((tokens, width), BF)
    dma = pltpu.SemaphoreType.DMA
    cot_shape = (pieces, count * tokens, piece)
    arr_shape = (EXP_DEV, units, count * tokens)
    scratch = [
        pltpu.VMEM((count, EXP_DEV, units, tokens), BF),
        pltpu.VMEM((2, width, head), BF),
        pltpu.VMEM((inner, 2, width, head), BF),
        pltpu.VMEM((2, width, head), F32),
        pltpu.VMEM((2, width, head), BF),
        pltpu.VMEM((2, width, head), BF),
        pltpu.VMEM((2, width, head), F32),
        pltpu.VMEM((HEADS, tokens, tokens), BF),
        pltpu.VMEM((HEADS, tokens, tokens), BF),
        dma((pieces, count, inner + 1)), dma((pieces, count)),
        dma((count,)), dma((count,)),
        dma((inner,)), dma((inner,)),
        dma((2,)), dma((2,)),
        dma((1 + pieces,)),
    ]
    if fused:
        out_shape = (flat,) * 4 + (jax.ShapeDtypeStruct((EXP_DEV, quarter, width), BF),)
        out_specs = (vmem,) * 5
        far = (pieces, chips - 1, EXP_DEV, quarter, piece)
        scratch = [pltpu.VMEM(cot_shape, BF), pltpu.VMEM(arr_shape, BF)] + scratch + [
            pltpu.VMEM((pieces, EXP_DEV, groups, quarter, piece), BF),
            pltpu.VMEM((pieces, EXP_DEV, chips, quarter, piece), BF),
            pltpu.VMEM(far, BF), pltpu.VMEM(far, BF),
            dma((pieces, chips)), dma((pieces, chips)),
            dma((pieces, chips - 1)), dma((pieces, chips - 1)),
        ]
    else:
        out_shape = (flat,) * 4 + (
            jax.ShapeDtypeStruct(cot_shape, BF), jax.ShapeDtypeStruct(arr_shape, BF)
        )
        out_specs = (vmem,) * 4 + (anywhere,) * 2
    result = pl.pallas_call(
        functools.partial(exchange_kernel, inner, pieces, fused),
        out_shape=out_shape,
        in_specs=[vmem] * 6,
        out_specs=out_specs,
        scratch_shapes=scratch,
        compiler_params=pltpu.CompilerParams(
            collective_id=0, has_side_effects=True, vmem_limit_bytes=VMEM_BYTES
        ),
        name="exchange",
    )(query, key_in, value, cotangent, hidden, routes)
    if fused:
        return result
    *heads, all_cot, arrived = result
    term = jnp.einsum("xft,td->xfd", arrived, all_cot[0], preferred_element_type=F32)
    expert_grad = lax.psum_scatter(term.astype(BF), "grp", scatter_dimension=1, tiled=True)
    return (*heads, expert_grad)


def per_device(query, key_in, value, cotangent, routes, gates, hidden):
    scaled = (gates[0][:, :, None] * hidden[0].astype(F32)).astype(BF).transpose(1, 2, 0)
    outputs, grad_q, grad_k, grad_v, expert_grad = exchange(
        query[0], key_in[0], value[0], cotangent[0], scaled, routes[0].T
    )
    return (outputs[None], grad_q[None], grad_k[None], grad_v[None], expert_grad)


def solution(mesh):
    rows = P("grp", "seq", None)
    in_specs = (rows, rows, rows, rows, rows, rows, P("grp", "seq", None, None))
    out_specs = (rows, rows, rows, rows, P("seq", "grp", None))
    return jax.shard_map(
        per_device, mesh=mesh, in_specs=in_specs, out_specs=out_specs, check_vma=False
    )
```
